32 devices in a mesh: blk: 8 (over z, core), head: 4 (over y, x).
Axes of the slice: x: 2, y: 2, z: 4, core: 2. Of those that a mesh axis runs over, the one named last changes fastest.
Arguments:
- queries: bfloat16 [8192, 4096], P(('blk', 'head')), may hold values from -60 to 60
- keys: bfloat16 [8192, 4096], P(('blk', 'head')), may hold values from -6.5 to 6.5
- values: bfloat16 [8192, 4096], P(('blk', 'head')), may hold values from -6 to 6
- block_lists: int32 [32, 3], P('blk'), may hold values from 0 to 31, as said below
- block_counts: int32 [32], P('blk'), may hold values from 1 to 3, as said below
Outputs:
- attended: bfloat16 [8192, 4096], P(('blk', 'head'))
The draws below stay inside these ranges and needn't reach their ends.
Inputs may be any that keep to these rules, and one draw needn't show every extreme that they name: `block_lists`: row q holds distinct block indices among q - 2 to q, none below 0, starting with q itself; only its first block_counts[q] entries are used, and the rest repeat q. block_counts[q] is at most min(q + 1, 3); the last block's count is 3.
All inputs are finite; a program needn't handle non-finite values.
Results may differ from the reference program's by a relative error of at most 0.0037.
Values may be sent and summed in bfloat16 or wider, within the bound.
A program may use at most 64 MiB of HBM per device.

```python
import jax
import jax.numpy as jnp
from jax import lax

HEADS = 32
HDIM = 128
BLOCK = 256
CYCLE = 3
D = 4096
NBLK = 32
FRAMES = 8192


def sparse_pattern(key):
    first_key = jax.random.fold_in(key, 11)
    second_key = jax.random.fold_in(key, 12)
    rows = jnp.arange(NBLK, dtype=jnp.int32)[:, None]
    dist = jnp.arange(CYCLE, dtype=jnp.int32)[None, :]
    raw = jax.random.randint(first_key, (NBLK, CYCLE), 0, 4096, dtype=jnp.int32)
    score = jnp.where(dist == 0, 4096 * CYCLE * 2, raw * CYCLE + dist)
    score = jnp.where(dist <= rows, score, -1)
    order = jnp.argsort(-score, axis=1).astype(jnp.int32)
    drawn = jax.random.randint(second_key, (NBLK,), 1, CYCLE + 1, dtype=jnp.int32)
    counts = jnp.minimum(drawn, rows[:, 0] + 1)
    counts = jnp.where(jnp.arange(NBLK, dtype=jnp.int32) == NBLK - 1, CYCLE, counts).astype(jnp.int32)
    lists = jnp.where(dist < counts[:, None], rows - order, rows).astype(jnp.int32)
    return (lists, counts)


def draw_block_lists(key, part):
    return sparse_pattern(key)[0]


def draw_block_counts(key, part):
    return sparse_pattern(key)[1]


def key_base(key):
    base_key = jax.random.fold_in(key, 21)
    return jnp.clip(jax.random.normal(base_key, (FRAMES, D), jnp.float32), -6.0, 6.0)


def draw_keys(key, part):
    base = key_base(key)
    return base.astype(jnp.bfloat16)


def draw_queries(key, part):
    query_key = jax.random.fold_in(key, 23)
    base = jnp.clip(jax.random.normal(query_key, (FRAMES, D), jnp.float32), -6.0, 6.0)
    return base.astype(jnp.bfloat16)


def steps_of(key, extent, split, least, high):
    gain = 1.0
    for axis_at, parts in split:
        draws = jax.random.uniform(jax.random.fold_in(jax.random.fold_in(key, 6), axis_at), (parts,), jnp.float32, least / len(split), high / len(split))
        gain = gain * jnp.repeat(jnp.exp(draws), extent[axis_at] // parts).reshape((-1,) + (1,) * (len(extent) - 1 - axis_at))
    return gain


def gaussian(rng, shape, deviation, limit, cuts=(), kind=jnp.bfloat16):
    values = deviation * jax.random.normal(rng, shape, jnp.float32)
    if cuts:
        values = values * steps_of(rng, shape, cuts, -0.22, 0.18)
    return jnp.clip(values, -limit, limit).astype(kind)


def setup_inputs(seed: int = 0) -> dict:
    seeds = jax.random.split(jax.random.key(seed), 6)
    queries = draw_queries(jax.random.fold_in(seeds[5], 71), 0)
    keys = draw_keys(jax.random.fold_in(seeds[5], 71), 0)
    values = gaussian(seeds[2], (FRAMES, D), 1.0, 6.0, ((0, 32),))
    block_lists = draw_block_lists(jax.random.fold_in(seeds[5], 71), 0)
    block_counts = draw_block_counts(jax.random.fold_in(seeds[5], 71), 0)
    return dict(queries=queries, keys=keys, values=values, block_lists=block_lists, block_counts=block_counts)


def reference(queries, keys, values, block_lists, block_counts):
    nblk = FRAMES // BLOCK
    scale = 1.0 / (HDIM ** 0.5)
    qall = queries.reshape(nblk, BLOCK, HEADS, HDIM)
    kall = keys.reshape(nblk, BLOCK, HEADS, HDIM)
    vall = values.reshape(nblk, BLOCK, HEADS, HDIM)

    def one_block(index):
        qblock = lax.dynamic_index_in_dim(qall, index, 0, keepdims=False).astype(jnp.float32)
        picks = lax.dynamic_index_in_dim(block_lists, index, 0, keepdims=False).astype(jnp.int32)
        count = lax.dynamic_index_in_dim(block_counts, index, 0, keepdims=False)
        kblock = kall[picks].reshape(CYCLE * BLOCK, HEADS, HDIM).astype(jnp.float32)
        vblock = vall[picks].reshape(CYCLE * BLOCK, HEADS, HDIM).astype(jnp.float32)
        valid = jnp.arange(CYCLE, dtype=jnp.int32) < count
        key_frame = (picks[:, None] * BLOCK + jnp.arange(BLOCK, dtype=jnp.int32)[None, :]).reshape(-1)
        query_frame = index * BLOCK + jnp.arange(BLOCK, dtype=jnp.int32)
        mask = jnp.repeat(valid, BLOCK)[None, :] & (key_frame[None, :] <= query_frame[:, None])
        scores = jnp.einsum("qhd,khd->hqk", qblock, kblock) * scale
        scores = jnp.where(mask[None], scores, -1e30)
        top = jnp.max(scores, axis=-1, keepdims=True)
        weights = jnp.where(mask[None], jnp.exp(scores - top), 0.0)
        total = jnp.sum(weights, axis=-1)
        rounded = lax.optimization_barrier(weights.astype(jnp.bfloat16)).astype(jnp.float32)
        summed = jnp.einsum("hqk,khd->qhd", rounded, vblock)
        result = summed / jnp.transpose(total)[:, :, None]
        return result.reshape(BLOCK, HEADS * HDIM).astype(jnp.bfloat16)

    blocks = lax.map(one_block, jnp.arange(nblk, dtype=jnp.int32))
    return blocks.reshape(FRAMES, HEADS * HDIM)
```

```python
import functools
import math

import jax
import jax.numpy as jnp
from jax import lax
from jax.experimental import pallas as pl
from jax.experimental.pallas import tpu as pltpu
from jax.sharding import PartitionSpec as P

HEADS = 32
HDIM = 128
BLOCK = 256
CYCLE = 3

MESH = pl.DeviceIdType.MESH
CHUNK = 2
WINDOW = 4
LOW = -1e30


def from_behind(value, axis, steps):
    count = lax.axis_size(axis)
    initial, last = (max(0, -steps), min(count, count - steps))
    return lax.ppermute(value, axis, [(source, source + steps) for source in range(initial, last)])


def by_heads(queries, keys, values, block_lists, block_counts):
    local_heads = HEADS // lax.axis_size("head")
    scale = 1.0 / HDIM**0.5
    qmine = lax.all_to_all(queries, "head", split_axis=1, concat_axis=0, tiled=True)
    kmine, vmine = (
        lax.all_to_all(keys, "head", split_axis=1, concat_axis=0, tiled=True),
        lax.all_to_all(values, "head", split_axis=1, concat_axis=0, tiled=True),
    )
    rows = qmine.shape[0]
    owned_blocks = rows // BLOCK
    reach = CYCLE - 1
    mine = jnp.stack((kmine, vmine))
    before = from_behind(mine, "blk", 1)[:, rows - reach * BLOCK :]
    extended = jnp.concatenate((before, mine), axis=1)
    own = lax.axis_index("blk")
    entry = jnp.arange(CYCLE, dtype=jnp.int32)
    frame_pos = jnp.arange(BLOCK, dtype=jnp.int32)
    causal = frame_pos[None, :] <= frame_pos[:, None]
    outputs = []
    for local in range(owned_blocks):
        target = own * owned_blocks + local
        list_row = block_lists[local]
        count = block_counts[local]
        used = entry < count
        parts_mask = []
        for place in range(CYCLE):
            distance = reach - place
            wanted = jnp.any(used & (list_row == target - distance))
            if distance == 0:
                parts_mask.append(causal & wanted)
            else:
                parts_mask.append(jnp.broadcast_to(wanted, (BLOCK, BLOCK)))
        mask = jnp.concatenate(parts_mask, axis=1)
        span = extended[:, local * BLOCK : (local + CYCLE) * BLOCK]
        qsplit = qmine[local * BLOCK : (local + 1) * BLOCK].reshape(BLOCK, local_heads, HDIM)
        ksplit = span[0].reshape(CYCLE * BLOCK, local_heads, HDIM)
        vsplit = span[1].reshape(CYCLE * BLOCK, local_heads, HDIM)
        scores = (
            jnp.einsum("qhd,khd->hqk", qsplit, ksplit, preferred_element_type=jnp.float32) * scale
        )
        scores = jnp.where(mask[None], scores, -1e30)
        top = jnp.max(scores, axis=-1, keepdims=True)
        weights = jnp.where(mask[None], jnp.exp(scores - top), 0.0)
        total = jnp.sum(weights, axis=-1)
        rounded = weights.astype(jnp.bfloat16)
        summed = jnp.einsum("hqk,khd->qhd", rounded, vsplit, preferred_element_type=jnp.float32)
        result = summed / jnp.transpose(total)[:, :, None]
        outputs.append(result.reshape(BLOCK, local_heads * HDIM).astype(jnp.bfloat16))
    joined = jnp.concatenate(outputs, axis=0)
    return lax.all_to_all(joined, "head", split_axis=0, concat_axis=1, tiled=True)


def kernel(
    width, runs, chunk, window,
    lists, counts, queries, keys, values, out,
    q_mine, k_mine, v_mine, one_k, one_v, two_k, two_v, o_mine,
    local_sem, out_sem, far_send, far_recv, near_send, near_recv,
):
    across = chunk * HDIM
    chunks = HEADS // chunk
    blk, head = lax.axis_index("blk"), lax.axis_index("head")
    me = blk * width + head
    total = runs * width
    even = lax.rem(head, 2) == 0

    def at(step):
        moved = me + step
        return (lax.div(moved, width), lax.rem(moved, width))

    ahead, behind = me + 2 < total, me >= 2
    passes = jnp.logical_or(even, me >= 3)
    partner = (blk, jnp.where(even, head + 1, head - 1))

    barrier = pltpu.get_barrier_semaphore()
    pl.semaphore_signal(barrier, inc=1, device_id=partner, device_id_type=MESH)

    @pl.when(ahead)
    def _():
        pl.semaphore_signal(barrier, inc=1, device_id=at(2), device_id_type=MESH)

    @pl.when(behind)
    def _():
        pl.semaphore_signal(barrier, inc=1, device_id=at(-2), device_id_type=MESH)

    loads = [
        pltpu.make_async_copy(source, target, local_sem.at[i])
        for i, (source, target) in enumerate(((queries, q_mine), (keys, k_mine), (values, v_mine)))
    ]
    for load in loads:
        load.start()

    pl.semaphore_wait(barrier, 1 + ahead.astype(jnp.int32) + behind.astype(jnp.int32))

    def columns(c):
        return pl.ds(pl.multiple_of(c * across, across), across)

    def far(c):
        return [
            pltpu.make_async_remote_copy(
                src_ref=source.at[:, columns(c)], dst_ref=target.at[c],
                send_sem=far_send.at[i, c], recv_sem=far_recv.at[i, c],
                device_id=at(2), device_id_type=MESH,
            )
            for i, (source, target) in enumerate(((keys, two_k), (values, two_v)))
        ]

    def near_own(c):
        return [
            pltpu.make_async_remote_copy(
                src_ref=source.at[:, columns(c)], dst_ref=target.at[c],
                send_sem=near_send.at[i, c], recv_sem=near_recv.at[i, c],
                device_id=partner, device_id_type=MESH,
            )
            for i, (source, target) in enumerate(((keys, one_k), (values, one_v)))
        ]

    def near_pass(c):
        return [
            pltpu.make_async_remote_copy(
                src_ref=source.at[c], dst_ref=target.at[c],
                send_sem=near_send.at[i, c], recv_sem=near_recv.at[i, c],
                device_id=partner, device_id_type=MESH,
            )
            for i, (source, target) in enumerate(((two_k, one_k), (two_v, one_v)))
        ]

    def send_own(c):
        far_copies, near_copies = far(c), near_own(c)
        for i in range(2):
            @pl.when(ahead)
            def _():
                far_copies[i].start()

            @pl.when(even)
            def _():
                near_copies[i].start()

    for c in range(window):
        send_own(c)

    @pl.when(jnp.logical_not(behind))
    def _():
        two_k[...] = jnp.zeros_like(two_k)
        two_v[...] = jnp.zeros_like(two_v)

    @pl.when(me == 0)
    def _():
        one_k[...] = jnp.zeros_like(one_k)
        one_v[...] = jnp.zeros_like(one_v)

    def wanted(distance):
        found = False
        for place in range(CYCLE):
            hit = jnp.logical_and(place < counts[head], lists[head, place] == me - distance)
            found = jnp.logical_or(found, hit)
        return found

    shape = (BLOCK, BLOCK)
    causal = lax.broadcasted_iota(jnp.int32, shape, 1) <= lax.broadcasted_iota(jnp.int32, shape, 0)
    bias_own = jnp.where(jnp.logical_and(causal, wanted(0)), 0.0, LOW)
    bias_one = jnp.where(wanted(1), 0.0, LOW)
    bias_two = jnp.where(wanted(2), 0.0, LOW)
    rate = math.log2(math.e) / math.sqrt(HDIM)

    for load in loads:
        load.wait()

    def attend(c):
        for h in range(chunk):
            mine = pl.ds(pl.multiple_of(c * across + h * HDIM, HDIM), HDIM)
            held = slice(h * HDIM, (h + 1) * HDIM)
            q = q_mine[:, mine]

            def score(k):
                return lax.dot_general(q, k, (((1,), (1,)), ((), ())), preferred_element_type=jnp.float32)

            own = score(k_mine[:, mine]) + bias_own
            one = score(one_k[c, :, held])
            two = score(two_k[c, :, held])
            top = jnp.maximum(
                jnp.max(own, axis=1, keepdims=True),
                jnp.maximum(
                    jnp.max(one, axis=1, keepdims=True) + bias_one,
                    jnp.max(two, axis=1, keepdims=True) + bias_two,
                ),
            )
            own = jnp.exp2((own - top) * rate)
            one = jnp.exp2((one - (top - bias_one)) * rate)
            two = jnp.exp2((two - (top - bias_two)) * rate)
            weight = jnp.sum(own + one + two, axis=1, keepdims=True)

            def part(w, v):
                return jnp.dot(w.astype(jnp.bfloat16), v, preferred_element_type=jnp.float32)

            summed = part(own, v_mine[:, mine]) + part(one, one_v[c, :, held]) + part(two, two_v[c, :, held])
            o_mine[:, mine] = (summed / weight).astype(o_mine.dtype)

    def result(c):
        return pltpu.make_async_copy(o_mine.at[:, columns(c)], out.at[:, columns(c)], out_sem.at[c])

    def step(c, carry):
        far_copies, passed = far(c), near_pass(c)
        for i in range(2):
            @pl.when(behind)
            def _():
                far_copies[i].wait_recv()

            @pl.when(jnp.logical_and(jnp.logical_not(even), behind & passes))
            def _():
                passed[i].start()

        @pl.when(ahead)
        def _():
            for copy in far_copies:
                copy.wait_send()

        @pl.when(even)
        def _():
            for copy in near_own(c):
                copy.wait_send()

        @pl.when(c + window < chunks)
        def _():
            send_own(c + window)

        @pl.when(me >= 1)
        def _():
            for copy in passed:
                copy.wait_recv()

        attend(c)
        result(c).start()
        return carry

    lax.fori_loop(0, chunks, step, 0)

    def finish(c, carry):
        result(c).wait()

        @pl.when(jnp.logical_and(jnp.logical_not(even), passes))
        def _():
            for copy in near_pass(c):
                copy.wait_send()

        return carry

    lax.fori_loop(0, chunks, finish, 0)


def by_blocks(width, runs, queries, keys, values, block_lists, block_counts):
    chunks = HEADS // CHUNK
    across = CHUNK * HDIM
    whole = pltpu.VMEM(queries.shape, jnp.bfloat16)
    landing = pltpu.VMEM((chunks, BLOCK, across), jnp.bfloat16)
    return pl.pallas_call(
        functools.partial(kernel, width, runs, CHUNK, min(WINDOW, chunks)),
        out_shape=jax.ShapeDtypeStruct(queries.shape, jnp.bfloat16),
        in_specs=[pl.BlockSpec(memory_space=pltpu.SMEM)] * 2 + [pl.BlockSpec(memory_space=pl.ANY)] * 3,
        out_specs=pl.BlockSpec(memory_space=pl.ANY),
        scratch_shapes=[
            whole, whole, whole, landing, landing, landing, landing, whole,
            pltpu.SemaphoreType.DMA((3,)),
            pltpu.SemaphoreType.DMA((chunks,)),
            pltpu.SemaphoreType.DMA((2, chunks)),
            pltpu.SemaphoreType.DMA((2, chunks)),
            pltpu.SemaphoreType.DMA((2, chunks)),
            pltpu.SemaphoreType.DMA((2, chunks)),
        ],
        compiler_params=pltpu.CompilerParams(
            collective_id=0, has_side_effects=True, vmem_limit_bytes=40 * 2**20
        ),
    )(block_lists, block_counts, queries, keys, values)


def solution(mesh):
    width, runs = mesh.shape["head"], mesh.shape["blk"]

    def body(queries, keys, values, block_lists, block_counts):
        if queries.shape[0] == BLOCK and width % 2 == 0:
            return by_blocks(width, runs, queries, keys, values, block_lists, block_counts)
        return by_heads(queries, keys, values, block_lists, block_counts)

    return jax.shard_map(
        body,
        mesh=mesh,
        in_specs=(
            P(("blk", "head"), None),
            P(("blk", "head"), None),
            P(("blk", "head"), None),
            P("blk", None),
            P("blk"),
        ),
        out_specs=P(("blk", "head"), None),
        check_vma=False,
    )
```

```python
import functools
import math

import jax
import jax.numpy as jnp
from jax import lax
from jax.experimental import pallas as pl
from jax.experimental.pallas import tpu as pltpu
from jax.sharding import PartitionSpec as P

HEADS = 32
HDIM = 128
BLOCK = 256
CYCLE = 3

MESH = pl.DeviceIdType.MESH
CHUNK = 2
FARW = 1
NEARW = 1
LAG = 1
LOW = -1e30
VMEM = 67108864


def from_behind(value, axis, steps):
    count = lax.axis_size(axis)
    initial, last = (max(0, -steps), min(count, count - steps))
    return lax.ppermute(value, axis, [(source, source + steps) for source in range(initial, last)])


def by_heads(queries, keys, values, block_lists, block_counts):
    local_heads = HEADS // lax.axis_size("head")
    scale = 1.0 / HDIM**0.5
    qmine = lax.all_to_all(queries, "head", split_axis=1, concat_axis=0, tiled=True)
    kmine, vmine = (
        lax.all_to_all(keys, "head", split_axis=1, concat_axis=0, tiled=True),
        lax.all_to_all(values, "head", split_axis=1, concat_axis=0, tiled=True),
    )
    rows = qmine.shape[0]
    owned_blocks = rows // BLOCK
    reach = CYCLE - 1
    mine = jnp.stack((kmine, vmine))
    before = from_behind(mine, "blk", 1)[:, rows - reach * BLOCK :]
    extended = jnp.concatenate((before, mine), axis=1)
    own = lax.axis_index("blk")
    entry = jnp.arange(CYCLE, dtype=jnp.int32)
    frame_pos = jnp.arange(BLOCK, dtype=jnp.int32)
    causal = frame_pos[None, :] <= frame_pos[:, None]
    outputs = []
    for local in range(owned_blocks):
        target = own * owned_blocks + local
        list_row = block_lists[local]
        count = block_counts[local]
        used = entry < count
        parts_mask = []
        for place in range(CYCLE):
            distance = reach - place
            wanted = jnp.any(used & (list_row == target - distance))
            if distance == 0:
                parts_mask.append(causal & wanted)
            else:
                parts_mask.append(jnp.broadcast_to(wanted, (BLOCK, BLOCK)))
        mask = jnp.concatenate(parts_mask, axis=1)
        span = extended[:, local * BLOCK : (local + CYCLE) * BLOCK]
        qsplit = qmine[local * BLOCK : (local + 1) * BLOCK].reshape(BLOCK, local_heads, HDIM)
        ksplit = span[0].reshape(CYCLE * BLOCK, local_heads, HDIM)
        vsplit = span[1].reshape(CYCLE * BLOCK, local_heads, HDIM)
        scores = (
            jnp.einsum("qhd,khd->hqk", qsplit, ksplit, preferred_element_type=jnp.float32) * scale
        )
        scores = jnp.where(mask[None], scores, -1e30)
        top = jnp.max(scores, axis=-1, keepdims=True)
        weights = jnp.where(mask[None], jnp.exp(scores - top), 0.0)
        total = jnp.sum(weights, axis=-1)
        rounded = weights.astype(jnp.bfloat16)
        summed = jnp.einsum("hqk,khd->qhd", rounded, vsplit, preferred_element_type=jnp.float32)
        result = summed / jnp.transpose(total)[:, :, None]
        outputs.append(result.reshape(BLOCK, local_heads * HDIM).astype(jnp.bfloat16))
    joined = jnp.concatenate(outputs, axis=0)
    return lax.all_to_all(joined, "head", split_axis=0, concat_axis=1, tiled=True)


def kernel(
    width, runs, chunk, far_window, near_window, lag,
    lists_far, counts_far, queries, keys, values, out,
    lists, counts, q_mine, k_mine, v_mine, one_k, one_v, two_k, two_v, o_mine,
    local_sem, out_sem, far_send, far_recv, near_send, near_recv,
):
    across = chunk * HDIM
    chunks = HEADS // chunk
    blk, head = lax.axis_index("blk"), lax.axis_index("head")
    me = blk * width + head
    total = runs * width
    even = lax.rem(head, 2) == 0

    def at(step):
        moved = me + step
        return (lax.div(moved, width), lax.rem(moved, width))

    ahead, behind = me + 2 < total, me >= 2
    partner = (blk, jnp.where(even, head + 1, head - 1))

    barrier = pltpu.get_barrier_semaphore()
    pl.semaphore_signal(barrier, inc=1, device_id=partner, device_id_type=MESH)

    @pl.when(ahead)
    def _():
        pl.semaphore_signal(barrier, inc=1, device_id=at(2), device_id_type=MESH)

    @pl.when(behind)
    def _():
        pl.semaphore_signal(barrier, inc=1, device_id=at(-2), device_id_type=MESH)

    loads = [
        pltpu.make_async_copy(source, target, local_sem.at[i])
        for i, (source, target) in enumerate((
            (lists_far, lists), (counts_far, counts), (queries, q_mine), (keys, k_mine), (values, v_mine)
        ))
    ]
    for load in loads:
        load.start()

    pl.semaphore_wait(barrier, 1 + ahead.astype(jnp.int32) + behind.astype(jnp.int32))

    def columns(c):
        return pl.ds(pl.multiple_of(c * across, across), across)

    def far(c):
        return [
            pltpu.make_async_remote_copy(
                src_ref=source.at[:, columns(c)], dst_ref=target.at[c],
                send_sem=far_send.at[i, c], recv_sem=far_recv.at[i, c],
                device_id=at(2), device_id_type=MESH,
            )
            for i, (source, target) in enumerate(((keys, two_k), (values, two_v)))
        ]

    def near_own(c):
        return [
            pltpu.make_async_remote_copy(
                src_ref=source.at[:, columns(c)], dst_ref=target.at[c],
                send_sem=near_send.at[i, c], recv_sem=near_recv.at[i, c],
                device_id=partner, device_id_type=MESH,
            )
            for i, (source, target) in enumerate(((keys, one_k), (values, one_v)))
        ]

    def near_pass(c):
        return [
            pltpu.make_async_remote_copy(
                src_ref=source.at[c], dst_ref=target.at[c],
                send_sem=near_send.at[i, c], recv_sem=near_recv.at[i, c],
                device_id=partner, device_id_type=MESH,
            )
            for i, (source, target) in enumerate(((two_k, one_k), (two_v, one_v)))
        ]

    def send_far(c):
        @pl.when(ahead)
        def _():
            for copy in far(c):
                copy.start()

    def send_near(c):
        @pl.when(even)
        def _():
            for copy in near_own(c):
                copy.start()

    for c in range(max(far_window, near_window)):
        if c < far_window:
            send_far(c)
        if c < near_window:
            send_near(c)

    @pl.when(jnp.logical_not(behind))
    def _():
        two_k[...] = jnp.zeros_like(two_k)
        two_v[...] = jnp.zeros_like(two_v)

    @pl.when(me == 0)
    def _():
        one_k[...] = jnp.zeros_like(one_k)
        one_v[...] = jnp.zeros_like(one_v)

    for load in loads:
        load.wait()

    def wanted(distance):
        found = False
        for place in range(CYCLE):
            hit = jnp.logical_and(place < counts[head], lists[head, place] == me - distance)
            found = jnp.logical_or(found, hit)
        return found

    shape = (BLOCK, BLOCK)
    causal = lax.broadcasted_iota(jnp.int32, shape, 1) <= lax.broadcasted_iota(jnp.int32, shape, 0)
    bias_own = jnp.where(jnp.logical_and(causal, wanted(0)), 0.0, LOW)
    bias_one = jnp.where(wanted(1), 0.0, LOW)
    bias_two = jnp.where(wanted(2), 0.0, LOW)
    rate = math.log2(math.e) / math.sqrt(HDIM)

    def attend(c):
        for h in range(chunk):
            mine = pl.ds(pl.multiple_of(c * across + h * HDIM, HDIM), HDIM)
            held = slice(h * HDIM, (h + 1) * HDIM)
            q = q_mine[:, mine]

            def score(k):
                return lax.dot_general(q, k, (((1,), (1,)), ((), ())), preferred_element_type=jnp.float32)

            own = score(k_mine[:, mine]) + bias_own
            one = score(one_k[c, :, held])
            two = score(two_k[c, :, held])
            top = jnp.maximum(
                jnp.max(own, axis=1, keepdims=True),
                jnp.maximum(
                    jnp.max(one, axis=1, keepdims=True) + bias_one,
                    jnp.max(two, axis=1, keepdims=True) + bias_two,
                ),
            )
            own = jnp.exp2((own - top) * rate)
            one = jnp.exp2((one - (top - bias_one)) * rate)
            two = jnp.exp2((two - (top - bias_two)) * rate)
            weight = jnp.sum(own + one + two, axis=1, keepdims=True)

            def part(w, v):
                return jnp.dot(w.astype(jnp.bfloat16), v, preferred_element_type=jnp.float32)

            summed = part(own, v_mine[:, mine]) + part(one, one_v[c, :, held]) + part(two, two_v[c, :, held])
            o_mine[:, mine] = (summed / weight).astype(o_mine.dtype)

    def result(c):
        return pltpu.make_async_copy(o_mine.at[:, columns(c)], out.at[:, columns(c)], out_sem.at[c])

    def move(c):
        far_copies, own, passed = far(c), near_own(c), near_pass(c)
        far_next, own_next = far(c + far_window), near_own(c + near_window)
        for i in range(2):
            @pl.when(behind)
            def _():
                far_copies[i].wait_recv()

            @pl.when(jnp.logical_and(jnp.logical_not(even), behind))
            def _():
                passed[i].start()

            @pl.when(ahead)
            def _():
                far_copies[i].wait_send()

            @pl.when(jnp.logical_and(ahead, c + far_window < chunks))
            def _():
                far_next[i].start()

            @pl.when(even)
            def _():
                own[i].wait_send()

            @pl.when(jnp.logical_and(even, c + near_window < chunks))
            def _():
                own_next[i].start()

    def work(c):
        @pl.when(me >= 1)
        def _():
            for copy in near_pass(c):
                copy.wait_recv()

        attend(c)
        result(c).start()

    def step(t, carry):
        @pl.when(t < chunks)
        def _():
            move(t)

        @pl.when(t >= lag)
        def _():
            work(t - lag)

        return carry

    lax.fori_loop(0, chunks + lag, step, 0)

    def finish(c, carry):
        result(c).wait()

        @pl.when(jnp.logical_and(jnp.logical_not(even), behind))
        def _():
            for copy in near_pass(c):
                copy.wait_send()

        return carry

    lax.fori_loop(0, chunks, finish, 0)


def by_blocks(width, runs, queries, keys, values, block_lists, block_counts):
    chunks = HEADS // CHUNK
    across = CHUNK * HDIM
    whole = pltpu.VMEM(queries.shape, jnp.bfloat16)
    landing = pltpu.VMEM((chunks, BLOCK, across), jnp.bfloat16)
    return pl.pallas_call(
        functools.partial(kernel, width, runs, CHUNK, FARW, NEARW, LAG),
        out_shape=jax.ShapeDtypeStruct(queries.shape, jnp.bfloat16),
        in_specs=[pl.BlockSpec(memory_space=pltpu.HBM)] * 5,
        out_specs=pl.BlockSpec(memory_space=pltpu.HBM),
        scratch_shapes=[
            pltpu.SMEM(block_lists.shape, jnp.int32), pltpu.SMEM(block_counts.shape, jnp.int32),
            whole, whole, whole, landing, landing, landing, landing, whole,
            pltpu.SemaphoreType.DMA((5,)),
            pltpu.SemaphoreType.DMA((chunks,)),
            pltpu.SemaphoreType.DMA((2, chunks)),
            pltpu.SemaphoreType.DMA((2, chunks)),
            pltpu.SemaphoreType.DMA((2, chunks)),
            pltpu.SemaphoreType.DMA((2, chunks)),
        ],
        compiler_params=pltpu.CompilerParams(
            collective_id=0, has_side_effects=True, vmem_limit_bytes=VMEM
        ),
    )(block_lists, block_counts, queries, keys, values)


def solution(mesh):
    width, runs = mesh.shape["head"], mesh.shape["blk"]

    def body(queries, keys, values, block_lists, block_counts):
        if queries.shape[0] == BLOCK and width % 2 == 0:
            return by_blocks(width, runs, queries, keys, values, block_lists, block_counts)
        return by_heads(queries, keys, values, block_lists, block_counts)

    return jax.shard_map(
        body,
        mesh=mesh,
        in_specs=(
            P(("blk", "head"), None),
            P(("blk", "head"), None),
            P(("blk", "head"), None),
            P("blk", None),
            P("blk"),
        ),
        out_specs=P(("blk", "head"), None),
        check_vma=False,
    )
```

```python
import functools
import math

import jax
import jax.numpy as jnp
from jax import lax
from jax.experimental import pallas as pl
from jax.experimental.pallas import tpu as pltpu
from jax.sharding import PartitionSpec as P

HEADS = 32
HDIM = 128
BLOCK = 256
CYCLE = 3

MESH = pl.DeviceIdType.MESH
CHUNK = 2
FARW = 1
NEARW = 1
LAG = 1
LOW = -1e30
VMEM = 67108864


def from_behind(value, axis, steps):
    count = lax.axis_size(axis)
    initial, last = (max(0, -steps), min(count, count - steps))
    return lax.ppermute(value, axis, [(source, source + steps) for source in range(initial, last)])


def by_heads(queries, keys, values, block_lists, block_counts):
    local_heads = HEADS // lax.axis_size("head")
    scale = 1.0 / HDIM**0.5
    qmine = lax.all_to_all(queries, "head", split_axis=1, concat_axis=0, tiled=True)
    kmine, vmine = (
        lax.all_to_all(keys, "head", split_axis=1, concat_axis=0, tiled=True),
        lax.all_to_all(values, "head", split_axis=1, concat_axis=0, tiled=True),
    )
    rows = qmine.shape[0]
    owned_blocks = rows // BLOCK
    reach = CYCLE - 1
    mine = jnp.stack((kmine, vmine))
    before = from_behind(mine, "blk", 1)[:, rows - reach * BLOCK :]
    extended = jnp.concatenate((before, mine), axis=1)
    own = lax.axis_index("blk")
    entry = jnp.arange(CYCLE, dtype=jnp.int32)
    frame_pos = jnp.arange(BLOCK, dtype=jnp.int32)
    causal = frame_pos[None, :] <= frame_pos[:, None]
    outputs = []
    for local in range(owned_blocks):
        target = own * owned_blocks + local
        list_row = block_lists[local]
        count = block_counts[local]
        used = entry < count
        parts_mask = []
        for place in range(CYCLE):
            distance = reach - place
            wanted = jnp.any(used & (list_row == target - distance))
            if distance == 0:
                parts_mask.append(causal & wanted)
            else:
                parts_mask.append(jnp.broadcast_to(wanted, (BLOCK, BLOCK)))
        mask = jnp.concatenate(parts_mask, axis=1)
        span = extended[:, local * BLOCK : (local + CYCLE) * BLOCK]
        qsplit = qmine[local * BLOCK : (local + 1) * BLOCK].reshape(BLOCK, local_heads, HDIM)
        ksplit = span[0].reshape(CYCLE * BLOCK, local_heads, HDIM)
        vsplit = span[1].reshape(CYCLE * BLOCK, local_heads, HDIM)
        scores = (
            jnp.einsum("qhd,khd->hqk", qsplit, ksplit, preferred_element_type=jnp.float32) * scale
        )
        scores = jnp.where(mask[None], scores, -1e30)
        top = jnp.max(scores, axis=-1, keepdims=True)
        weights = jnp.where(mask[None], jnp.exp(scores - top), 0.0)
        total = jnp.sum(weights, axis=-1)
        rounded = weights.astype(jnp.bfloat16)
        summed = jnp.einsum("hqk,khd->qhd", rounded, vsplit, preferred_element_type=jnp.float32)
        result = summed / jnp.transpose(total)[:, :, None]
        outputs.append(result.reshape(BLOCK, local_heads * HDIM).astype(jnp.bfloat16))
    joined = jnp.concatenate(outputs, axis=0)
    return lax.all_to_all(joined, "head", split_axis=0, concat_axis=1, tiled=True)


def kernel(
    width, runs, chunk, far_window, near_window, lag,
    lists_far, counts_far, queries, keys, values, out,
    lists, counts, q_mine, k_mine, v_mine, one_k, one_v, two_k, two_v, o_mine,
    local_sem, out_sem, far_send, far_recv, near_send, near_recv,
):
    across = chunk * HDIM
    chunks = HEADS // chunk
    blk, head = lax.axis_index("blk"), lax.axis_index("head")
    me = blk * width + head
    total = runs * width
    even = lax.rem(head, 2) == 0

    def at(step):
        moved = me + step
        return (lax.div(moved, width), lax.rem(moved, width))

    ahead, behind = me + 2 < total, me >= 2
    partner = (blk, jnp.where(even, head + 1, head - 1))

    barrier = pltpu.get_barrier_semaphore()
    pl.semaphore_signal(barrier, inc=1, device_id=partner, device_id_type=MESH)

    @pl.when(ahead)
    def _():
        pl.semaphore_signal(barrier, inc=1, device_id=at(2), device_id_type=MESH)

    @pl.when(behind)
    def _():
        pl.semaphore_signal(barrier, inc=1, device_id=at(-2), device_id_type=MESH)

    loads = [
        pltpu.make_async_copy(source, target, local_sem.at[i])
        for i, (source, target) in enumerate((
            (lists_far, lists), (counts_far, counts), (queries, q_mine), (keys, k_mine), (values, v_mine)
        ))
    ]
    for load in loads:
        load.start()

    pl.semaphore_wait(barrier, 1 + ahead.astype(jnp.int32) + behind.astype(jnp.int32))

    def columns(c):
        return pl.ds(pl.multiple_of(c * across, across), across)

    def far(c):
        return [
            pltpu.make_async_remote_copy(
                src_ref=source.at[:, columns(c)], dst_ref=target.at[c],
                send_sem=far_send.at[i, c], recv_sem=far_recv.at[i, c],
                device_id=at(2), device_id_type=MESH,
            )
            for i, (source, target) in enumerate(((keys, two_k), (values, two_v)))
        ]

    def near_own(c):
        return [
            pltpu.make_async_remote_copy(
                src_ref=source.at[:, columns(c)], dst_ref=target.at[c],
                send_sem=near_send.at[i, c], recv_sem=near_recv.at[i, c],
                device_id=partner, device_id_type=MESH,
            )
            for i, (source, target) in enumerate(((keys, one_k), (values, one_v)))
        ]

    def near_pass(c):
        return [
            pltpu.make_async_remote_copy(
                src_ref=source.at[c], dst_ref=target.at[c],
                send_sem=near_send.at[i, c], recv_sem=near_recv.at[i, c],
                device_id=partner, device_id_type=MESH,
            )
            for i, (source, target) in enumerate(((two_k, one_k), (two_v, one_v)))
        ]

    def send_far(c):
        @pl.when(ahead)
        def _():
            for copy in far(c):
                copy.start()

    def send_near(c):
        @pl.when(even)
        def _():
            for copy in near_own(c):
                copy.start()

    for c in range(max(far_window, near_window)):
        if c < far_window:
            send_far(c)
        if c < near_window:
            send_near(c)

    @pl.when(jnp.logical_not(behind))
    def _():
        two_k[...] = jnp.zeros_like(two_k)
        two_v[...] = jnp.zeros_like(two_v)

    @pl.when(me == 0)
    def _():
        one_k[...] = jnp.zeros_like(one_k)
        one_v[...] = jnp.zeros_like(one_v)

    for load in loads:
        load.wait()

    def wanted(distance):
        found = False
        for place in range(CYCLE):
            hit = jnp.logical_and(place < counts[head], lists[head, place] == me - distance)
            found = jnp.logical_or(found, hit)
        return found

    shape = (BLOCK, BLOCK)
    causal = lax.broadcasted_iota(jnp.int32, shape, 1) <= lax.broadcasted_iota(jnp.int32, shape, 0)
    bias_own = jnp.where(jnp.logical_and(causal, wanted(0)), 0.0, LOW)
    bias_one = jnp.where(wanted(1), 0.0, LOW)
    bias_two = jnp.where(wanted(2), 0.0, LOW)
    rate = math.log2(math.e) / math.sqrt(HDIM)

    def attend(c):
        for h in range(chunk):
            mine = pl.ds(pl.multiple_of(c * across + h * HDIM, HDIM), HDIM)
            held = slice(h * HDIM, (h + 1) * HDIM)
            q = q_mine[:, mine]

            def score(k):
                return lax.dot_general(q, k, (((1,), (1,)), ((), ())), preferred_element_type=jnp.float32)

            own = score(k_mine[:, mine]) + bias_own
            one = score(one_k[c, :, held])
            two = score(two_k[c, :, held])
            top = jnp.maximum(
                jnp.max(own, axis=1, keepdims=True),
                jnp.maximum(
                    jnp.max(one, axis=1, keepdims=True) + bias_one,
                    jnp.max(two, axis=1, keepdims=True) + bias_two,
                ),
            )
            own = jnp.exp2((own - top) * rate)
            one = jnp.exp2((one - (top - bias_one)) * rate)
            two = jnp.exp2((two - (top - bias_two)) * rate)
            weight = jnp.sum(own + one + two, axis=1, keepdims=True)

            def part(w, v):
                return jnp.dot(w.astype(jnp.bfloat16), v, preferred_element_type=jnp.float32)

            summed = part(own, v_mine[:, mine]) + part(one, one_v[c, :, held]) + part(two, two_v[c, :, held])
            o_mine[:, mine] = (summed / weight).astype(o_mine.dtype)

    def result(c):
        return pltpu.make_async_copy(o_mine.at[:, columns(c)], out.at[:, columns(c)], out_sem.at[c])

    def move(c):
        far_copies, own, passed = far(c), near_own(c), near_pass(c)
        far_next, own_next = far(c + far_window), near_own(c + near_window)
        for i in range(2):
            @pl.when(jnp.logical_and(jnp.logical_not(even), behind))
            def _():
                far_copies[i].wait_recv()
                passed[i].start()

            @pl.when(ahead)
            def _():
                far_copies[i].wait_send()

            @pl.when(jnp.logical_and(ahead, c + far_window < chunks))
            def _():
                far_next[i].start()

            @pl.when(even)
            def _():
                own[i].wait_send()

            @pl.when(jnp.logical_and(even, c + near_window < chunks))
            def _():
                own_next[i].start()

    def work(c):
        @pl.when(jnp.logical_and(even, behind))
        def _():
            for copy in far(c):
                copy.wait_recv()

        @pl.when(me >= 1)
        def _():
            for copy in near_pass(c):
                copy.wait_recv()

        attend(c)
        result(c).start()

    def step(t, carry):
        @pl.when(t < chunks)
        def _():
            move(t)

        @pl.when(t >= lag)
        def _():
            work(t - lag)

        return carry

    lax.fori_loop(0, chunks + lag, step, 0)

    def finish(c, carry):
        result(c).wait()

        @pl.when(jnp.logical_and(jnp.logical_not(even), behind))
        def _():
            for copy in near_pass(c):
                copy.wait_send()

        return carry

    lax.fori_loop(0, chunks, finish, 0)


def by_blocks(width, runs, queries, keys, values, block_lists, block_counts):
    chunks = HEADS // CHUNK
    across = CHUNK * HDIM
    whole = pltpu.VMEM(queries.shape, jnp.bfloat16)
    landing = pltpu.VMEM((chunks, BLOCK, across), jnp.bfloat16)
    return pl.pallas_call(
        functools.partial(kernel, width, runs, CHUNK, FARW, NEARW, LAG),
        out_shape=jax.ShapeDtypeStruct(queries.shape, jnp.bfloat16),
        in_specs=[pl.BlockSpec(memory_space=pltpu.HBM)] * 5,
        out_specs=pl.BlockSpec(memory_space=pltpu.HBM),
        scratch_shapes=[
            pltpu.SMEM(block_lists.shape, jnp.int32), pltpu.SMEM(block_counts.shape, jnp.int32),
            whole, whole, whole, landing, landing, landing, landing, whole,
            pltpu.SemaphoreType.DMA((5,)),
            pltpu.SemaphoreType.DMA((chunks,)),
            pltpu.SemaphoreType.DMA((2, chunks)),
            pltpu.SemaphoreType.DMA((2, chunks)),
            pltpu.SemaphoreType.DMA((2, chunks)),
            pltpu.SemaphoreType.DMA((2, chunks)),
        ],
        compiler_params=pltpu.CompilerParams(
            collective_id=0, has_side_effects=True, vmem_limit_bytes=VMEM
        ),
    )(block_lists, block_counts, queries, keys, values)


def solution(mesh):
    width, runs = mesh.shape["head"], mesh.shape["blk"]

    def body(queries, keys, values, block_lists, block_counts):
        if queries.shape[0] == BLOCK and width % 2 == 0:
            return by_blocks(width, runs, queries, keys, values, block_lists, block_counts)
        return by_heads(queries, keys, values, block_lists, block_counts)

    return jax.shard_map(
        body,
        mesh=mesh,
        in_specs=(
            P(("blk", "head"), None),
            P(("blk", "head"), None),
            P(("blk", "head"), None),
            P("blk", None),
            P("blk"),
        ),
        out_specs=P(("blk", "head"), None),
        check_vma=False,
    )
```
